256 devices in a mesh: sample: 64 (over y, x, z_lo, core), tensor: 4 (over z_hi).
Axes of the slice: x: 4, y: 4, z: 8 (z_hi: 4, z_lo: 2; z = z_hi * 2 + z_lo), core: 2. Of those that a mesh axis runs over, the one named last changes fastest.
Arguments:
- prompt_q: bfloat16 [8192, 4096], P('sample', 'tensor'), may hold values from -70 to 70
- prompt_k: bfloat16 [8192, 512], P('sample', 'tensor'), may hold values from -4 to 4
- prompt_v: bfloat16 [8192, 512], P('sample', 'tensor'), may hold values from -6 to 6
- suffix_q: bfloat16 [8192, 4096], P('sample', 'tensor'), may hold values from -70 to 70
- suffix_k: bfloat16 [8192, 512], P('sample', 'tensor'), may hold values from -4 to 4
- suffix_v: bfloat16 [8192, 512], P('sample', 'tensor'), may hold values from -6 to 6
- prompt_of: int32 [64], P('sample'), may hold values from 0 to 1
- suffix_len: int32 [64], P('sample'), may hold values from 1 to 128, 5120 in all
- out_weight: bfloat16 [4096, 8192], P('sample', 'tensor'), may hold values from -0.375 to 0.375
Outputs:
- prompt_out: bfloat16 [8192, 8192], P('sample', 'tensor')
- suffix_out: bfloat16 [8192, 8192], P('sample', 'tensor')
The draws below stay inside these ranges and needn't reach their ends.
Inputs may be any that keep to these rules, and one draw needn't show every extreme that they name: `suffix_len`: some suffix is exactly 128 long.
All inputs are finite; a program needn't handle non-finite values. No bound on the sum of `suffix_len` on one device may be relied on, other than what follows from the above.
Results may differ from the reference program's by a relative error of at most 0.0095.
Values may be sent and summed in bfloat16 or wider, within the bound.
No kernel may reach another device: no remote copies, remote signals or barrier semaphores. Data moves between devices by JAX's collectives and lax.ppermute only.
A program may use at most 64 MiB of HBM per device.

```python
import math
import jax
import jax.numpy as jnp
import numpy as np
from jax import lax

D = 8192
HD = 128
QH = 32
KVH = 4
PROMPTS = 2
SUF = 128
PROMPT_DEV = 128
SAMPLES = 64
PLEN = 4096
PTOK = 8192
STOK = 8192


def key_field(key, tag, rows, period):
    inner = jax.random.fold_in(key, tag)
    first_key = jax.random.fold_in(inner, 0)
    shaped = (rows, KVH * HD)
    field = jnp.clip(jax.random.normal(first_key, shaped, jnp.float32), -4.0, 4.0)
    placed = (jnp.arange(rows) % period == 5)[:, None]
    return jnp.where(placed, field, field)


def lean_queries(noise, rows, period):
    placed = (jnp.arange(rows) % period == 7)[:, None]
    return jnp.where(placed, noise, noise)


def draw_prompt_k(key, part):
    field = key_field(key, 1, PTOK, PROMPT_DEV)
    return field.astype(jnp.bfloat16)


def draw_prompt_q(key, part):
    own_key = jax.random.fold_in(key, 32)
    shaped = (PTOK, QH * HD)
    noise = 2.5 * jnp.clip(jax.random.normal(own_key, shaped, jnp.float32), -4.0, 4.0)
    result = lean_queries(noise, PTOK, PROMPT_DEV)
    return result.astype(jnp.bfloat16)


def draw_suffix_k(key, part):
    field = key_field(key, 2, STOK, SUF)
    return field.astype(jnp.bfloat16)


def draw_suffix_q(key, part):
    own_key = jax.random.fold_in(key, 34)
    shaped = (STOK, QH * HD)
    noise = 2.5 * jnp.clip(jax.random.normal(own_key, shaped, jnp.float32), -4.0, 4.0)
    result = lean_queries(noise, STOK, SUF)
    return result.astype(jnp.bfloat16)


def place_ends(drawn, key, least, top_value):
    longest = drawn.shape.index(max(drawn.shape))
    spots = []
    for shift in (0, 1):
        where = [jax.random.randint(jax.random.fold_in(key, axis), (), 0, length) for axis, length in enumerate(drawn.shape)]
        where[longest] = (where[longest] + shift) % drawn.shape[longest]
        spots.append(tuple(where))
    return drawn.at[spots[0]].set(least).at[spots[1]].set(top_value)


def shard_levels(key, shape, cuts, smallest, top_value):
    def one(axis_at, shards_of):
        draws = jax.random.uniform(jax.random.fold_in(jax.random.fold_in(key, 6), axis_at), (shards_of,), jnp.float32, smallest / len(cuts), top_value / len(cuts))
        return jnp.repeat(jnp.exp(draws), shape[axis_at] // shards_of).reshape((-1,) + (1,) * (len(shape) - axis_at - 1))

    factor_of = one(*cuts[0])
    for cut in cuts[1:]:
        factor_of = factor_of * one(*cut)
    return factor_of


def split_up(amount, total, limit, slope):
    weights = [(1 << 20) // math.isqrt(rank ** slope) + 1 for rank in range(2, amount + 1)]
    surplus, holding = total - limit - (amount - 1), [1] * (amount - 1)
    while surplus > 0:
        free = [i for i in range(amount - 1) if holding[i] < limit]
        pool, left = sum([weights[i] for i in free]), surplus
        for i in free:
            more = min(limit - holding[i], max(1, left * weights[i] // pool), surplus)
            holding[i] = holding[i] + more
            surplus = surplus - more
    return np.array([limit] + holding)


def uneven_parts(key, count, total, bound, slope):
    if count == 2:
        one = jax.random.randint(key, (), max(1, total - bound), min(bound, total - 1) + 1)
        return jnp.stack([one, total - one])
    tallies = jnp.asarray(split_up(count, total, bound, slope), jnp.int32)
    couples = (count - 1) // 2
    source_of, taker = tallies[1:1 + 2 * couples:2], tallies[2:2 + 2 * couples:2]
    room = jnp.minimum(source_of - 1, bound - taker)
    passed = jax.random.randint(jax.random.fold_in(key, 1), (couples,), 0, 1 << 20) % (room + 1)
    tallies = tallies.at[1:1 + 2 * couples:2].set(source_of - passed).at[2:2 + 2 * couples:2].set(taker + passed)
    return tallies[jax.random.permutation(jax.random.fold_in(key, 2), count)]


def gaussian(key, dims, scale, reach, shards=(), kind=jnp.bfloat16):
    values = scale * jax.random.normal(key, dims, jnp.float32)
    if shards:
        values = values * shard_levels(key, dims, shards, -0.22, 0.18)
    return jnp.clip(values, -reach, reach).astype(kind)


def setup_inputs(seed: int = 0) -> dict:
    key_of = jax.random.split(jax.random.key(seed), 10)
    return {
        "prompt_q": draw_prompt_q(jax.random.fold_in(key_of[9], 71), 0),
        "prompt_k": draw_prompt_k(jax.random.fold_in(key_of[9], 71), 0),
        "prompt_v": gaussian(key_of[2], (PTOK, KVH * HD), 1.0, 6.0, ((0, 64), (1, 4))),
        "suffix_q": draw_suffix_q(jax.random.fold_in(key_of[9], 71), 0),
        "suffix_k": draw_suffix_k(jax.random.fold_in(key_of[9], 71), 0),
        "suffix_v": gaussian(key_of[5], (STOK, KVH * HD), 1.0, 6.0, ((0, 64), (1, 4))),
        "prompt_of": place_ends(jax.random.randint(key_of[6], (SAMPLES,), 0, PROMPTS), jax.random.fold_in(key_of[6], 1), 0, PROMPTS - 1).astype(jnp.int32),
        "suffix_len": uneven_parts(key_of[7], SAMPLES, SAMPLES * SUF * 5 // 8, SUF, 1).astype(jnp.int32),
        "out_weight": gaussian(key_of[8], (QH * HD, D), (QH * HD // 16) ** -0.5, 0.375, ((0, 64), (1, 4))),
    }


def attend(queries, key_rows, value_rows, allowed):
    scale = queries.shape[-1] ** -0.5
    scores = jnp.einsum('hrd,kd->hrk', queries.astype(jnp.float32), key_rows.astype(jnp.float32)) * scale
    scores = jnp.where(allowed, scores, -1e30)
    largest = jnp.max(scores, axis=-1, keepdims=True)
    exps = jnp.where(allowed, jnp.exp(scores - largest), 0.0)
    totals = jnp.sum(exps, axis=-1, keepdims=True)
    rounded = lax.optimization_barrier(exps.astype(jnp.bfloat16)).astype(jnp.float32)
    return jnp.einsum('hrk,kd->hrd', rounded, value_rows.astype(jnp.float32)) / totals


def reference(prompt_q, prompt_k, prompt_v, suffix_q, suffix_k, suffix_v, prompt_of, suffix_len, out_weight):
    per_group = QH // KVH
    prompt_queries = prompt_q.reshape(PROMPTS, PLEN, KVH, per_group, HD).transpose(0, 2, 3, 1, 4).reshape(PROMPTS * KVH, per_group, PLEN, HD)
    prompt_keys = prompt_k.reshape(PROMPTS, PLEN, KVH, HD).transpose(0, 2, 1, 3)
    prompt_values = prompt_v.reshape(PROMPTS, PLEN, KVH, HD).transpose(0, 2, 1, 3)
    causal = jnp.arange(PLEN)[:, None] >= jnp.arange(PLEN)[None, :]

    def prompt_one(triple):
        return attend(triple[0], triple[1], triple[2], causal)

    prompt_heads = lax.map(prompt_one, (prompt_queries, prompt_keys.reshape(PROMPTS * KVH, PLEN, HD), prompt_values.reshape(PROMPTS * KVH, PLEN, HD)))
    prompt_attended = prompt_heads.reshape(PROMPTS, KVH, per_group, PLEN, HD).transpose(0, 3, 1, 2, 4).reshape(PTOK, QH * HD).astype(jnp.bfloat16)

    suffix_queries = suffix_q.reshape(SAMPLES, SUF, KVH, per_group, HD).transpose(0, 2, 3, 1, 4)
    suffix_keys = suffix_k.reshape(SAMPLES, SUF, KVH, HD).transpose(0, 2, 1, 3)
    suffix_values = suffix_v.reshape(SAMPLES, SUF, KVH, HD).transpose(0, 2, 1, 3)
    own_causal = jnp.arange(SUF)[:, None] >= jnp.arange(SUF)[None, :]
    allowed = jnp.concatenate([jnp.ones((SUF, PLEN), dtype=bool), own_causal], axis=1)

    def suffix_one(items):
        queries, own_keys, own_values, which, count = items
        key_rows = jnp.concatenate([prompt_keys[which], own_keys], axis=1)
        value_rows = jnp.concatenate([prompt_values[which], own_values], axis=1)
        result = jax.vmap(lambda aa, bb, cc: attend(aa, bb, cc, allowed))(queries, key_rows, value_rows)
        keep_rows = (jnp.arange(SUF) < count)[None, None, :, None]
        return jnp.where(keep_rows, result, 0.0)

    suffix_heads = lax.map(suffix_one, (suffix_queries, suffix_keys, suffix_values, prompt_of, suffix_len))
    suffix_attended = suffix_heads.transpose(0, 3, 1, 2, 4).reshape(STOK, QH * HD).astype(jnp.bfloat16)

    prompt_out = jnp.dot(prompt_attended, out_weight, preferred_element_type=jnp.float32).astype(jnp.bfloat16)
    suffix_out = jnp.dot(suffix_attended, out_weight, preferred_element_type=jnp.float32).astype(jnp.bfloat16)
    return prompt_out, suffix_out
```

```python
import functools

import jax
import jax.numpy as jnp
from jax import lax
from jax.experimental import pallas as pl
from jax.experimental.pallas import tpu as pltpu
from jax.sharding import PartitionSpec as P

HD = 128
HEADS = 8
ROWS = 128
PROMPTS = 2
SCALE = HD ** (-0.5) * 1.4426950408889634
ORDERS = ((4, 12, 16, 48), (12, 4, 48, 16), (16, 48, 4, 12), (48, 16, 12, 4))
VMEM = pl.BlockSpec(memory_space=pltpu.VMEM)
SMEM = pl.BlockSpec(memory_space=pltpu.SMEM)
ANY = pl.BlockSpec(memory_space=pl.ANY)


def slot_of(order, there, here):
    apart = there ^ here
    low_x, high_x = apart & 1, (apart >> 1) & 1
    low_y, high_y = (apart >> 2) & 1, (apart >> 3) & 1
    used = {4: low_x ^ high_x, 12: high_x, 16: low_y ^ high_y, 48: high_y}
    return sum(used[mask] << step for step, mask in enumerate(order))


def swap(x, mask):
    return lax.ppermute(x, "sample", [(s, s ^ mask) for s in range(64)])


def swap_tensor(x, mask):
    return lax.ppermute(x, "tensor", [(t, t ^ mask) for t in range(4)])


def gather_plane(pieces):
    for step in range(4):
        came = [swap(piece, order[step]) for piece, order in zip(pieces, ORDERS)]
        pieces = [jnp.concatenate([a, b], axis=0) for a, b in zip(pieces, came)]
    return pieces


def attend_kernel(is_prompt, info, q, own_k, own_v, *refs):
    blocks, (out, top, acc) = refs[:8], refs[8:]
    me = info[0]
    here = me >> 2
    row = lax.broadcasted_iota(jnp.int32, (ROWS, ROWS), 0)
    col = lax.broadcasted_iota(jnp.int32, (ROWS, ROWS), 1)
    ones = jnp.ones((ROWS, HD), jnp.bfloat16)
    keys = own_k[...]
    values = jnp.concatenate([own_v[...], ones], axis=1)
    for h in range(HEADS):
        scores = lax.dot_general(
            q[:, h * HD:(h + 1) * HD], keys, (((1,), (1,)), ((), ())),
            preferred_element_type=jnp.float32)
        scores = jnp.where(row >= col, scores, -1e30)
        best = jnp.broadcast_to(jnp.max(scores, axis=1, keepdims=True), (ROWS, HD))
        exps = jnp.exp2((scores - best) * SCALE).astype(jnp.bfloat16)
        top[h] = best
        acc[h] = jnp.dot(exps, values, preferred_element_type=jnp.float32)

    def absorb(chunk, masked):
        there = PROMPTS_SPAN * (info[0] >> 5 if is_prompt else info[1]) + chunk
        keys, values, allowed = [], [], []
        for rc in range(2):
            for rz in range(2):
                k_ref, v_ref = blocks[rc * 4 + rz * 2], blocks[rc * 4 + rz * 2 + 1]
                keys.append(k_ref[slot_of(ORDERS[rz * 2], there, here)])
                values.append(v_ref[slot_of(ORDERS[rz * 2 + 1], there, here)])
                allowed.append(((me ^ (rz * 2 + rc)) & 3) < (me & 3))
        keys = jnp.concatenate(keys, axis=0)
        values = jnp.concatenate(values, axis=0)
        values = jnp.concatenate([values, jnp.ones(values.shape, jnp.bfloat16)], axis=1)
        for h in range(HEADS):
            scores = lax.dot_general(
                q[:, h * HD:(h + 1) * HD], keys, (((1,), (1,)), ((), ())),
                preferred_element_type=jnp.float32)
            parts = [scores[:, i * ROWS:(i + 1) * ROWS] for i in range(4)]
            if masked:
                parts = [jnp.where(ok, part, -1e30) for ok, part in zip(allowed, parts)]
            best = jnp.maximum(jnp.maximum(parts[0], parts[1]), jnp.maximum(parts[2], parts[3]))
            old = top[h]
            new = jnp.maximum(old, jnp.max(best, axis=1, keepdims=True))
            shrink = jnp.exp2((old - new) * SCALE)
            exps = jnp.concatenate(
                [jnp.exp2((part - new) * SCALE).astype(jnp.bfloat16) for part in parts], axis=1)
            top[h] = new
            acc[h] = acc[h] * jnp.concatenate([shrink, shrink], axis=1) + jnp.dot(
                exps, values, preferred_element_type=jnp.float32)

    if is_prompt:
        whole = here & (PROMPTS_SPAN - 1)
        lax.fori_loop(0, whole, lambda i, c: (absorb(i, False), c)[1], 0)

        @pl.when((me & 3) > 0)
        def _():
            absorb(whole, True)
    else:
        lax.fori_loop(0, PROMPTS_SPAN, lambda i, c: (absorb(i, False), c)[1], 0)
    for h in range(HEADS):
        result = acc[h][:, :HD] / acc[h][:, HD:]
        if not is_prompt:
            result = jnp.where(row < info[2], result, 0.0)
        out[:, h * HD:(h + 1) * HD] = result.astype(jnp.bfloat16)


PROMPTS_SPAN = 16 // PROMPTS


def attend(is_prompt, info, q, own_k, own_v, blocks):
    return pl.pallas_call(
        functools.partial(attend_kernel, is_prompt),
        out_shape=jax.ShapeDtypeStruct((ROWS, HEADS * HD), jnp.bfloat16),
        in_specs=[SMEM] + [VMEM] * (3 + len(blocks)),
        out_specs=VMEM,
        scratch_shapes=[
            pltpu.VMEM((HEADS, ROWS, HD), jnp.float32),
            pltpu.VMEM((HEADS, ROWS, 2 * HD), jnp.float32),
        ],
        compiler_params=pltpu.CompilerParams(vmem_limit_bytes=40 << 20),
        name="attend_prompt" if is_prompt else "attend_suffix",
    )(info, q, own_k, own_v, *blocks)


def project_kernel(flip, last, *refs):
    if flip:
        info, a_p, a_s, total_in = refs[:4]
        refs = refs[4:]
    else:
        info, a_p, a_s = refs[:3]
        refs = refs[3:]
    weights, refs = refs[:8], refs[8:]
    if last:
        out_p, out_s, held, sems = refs
    else:
        total_out, held, sems = refs
    me = info[0]
    here = me >> 2
    quarter = info[3] ^ flip

    def copies(color):
        found = []
        for x in range(4):
            there = quarter * 4 + x
            slot = slot_of(ORDERS[color], there, here)
            for rz in range(2):
                for rc in range(2):
                    place = x * 4 + ((me ^ (rz * 2 + rc)) & 3)
                    found.append(pltpu.make_async_copy(
                        weights[rc * 4 + color].at[slot, rz],
                        held.at[color, pl.ds(pl.multiple_of(place * 64, 64), 64)],
                        sems.at[color, x * 4 + rz * 2 + rc]))
        return found

    for color in range(4):
        for copy in copies(color):
            copy.start()
    rows = jnp.concatenate([a_p[...], a_s[...]], axis=0)
    for color in range(4):
        for copy in copies(color):
            copy.wait()
        part = jnp.dot(rows, held[color], preferred_element_type=jnp.float32)
        lanes = slice(color * 512, (color + 1) * 512)
        if flip:
            part = part + total_in[:, lanes]
        if last:
            out_p[:, lanes] = part[:ROWS].astype(jnp.bfloat16)
            out_s[:, lanes] = part[ROWS:].astype(jnp.bfloat16)
        else:
            total_out[:, lanes] = part


def project(flip, last, info, a_p, a_s, weights, total):
    if last:
        out_shape = [jax.ShapeDtypeStruct((ROWS, 2048), jnp.bfloat16)] * 2
    else:
        out_shape = jax.ShapeDtypeStruct((2 * ROWS, 2048), jnp.float32)
    args = [info, a_p, a_s] + ([total] if flip else [])
    return pl.pallas_call(
        functools.partial(project_kernel, flip, last),
        out_shape=out_shape,
        in_specs=[SMEM] + [VMEM] * (len(args) - 1) + [ANY] * len(weights),
        out_specs=[VMEM] * 2 if last else VMEM,
        scratch_shapes=[
            pltpu.VMEM((4, 1024, 512), jnp.bfloat16),
            pltpu.SemaphoreType.DMA((4, 16)),
        ],
        compiler_params=pltpu.CompilerParams(vmem_limit_bytes=40 << 20),
        name="project_%d" % flip,
    )(*args, *weights)


def spread(a):
    from_1 = swap_tensor(a, 1)
    from_3 = swap_tensor(a, 3)
    left = swap_tensor(from_1[:, :512], 3)
    right = swap_tensor(from_3[:, 512:], 1)
    return from_1, from_3, jnp.concatenate([left, right], axis=1)


def per_device(
    prompt_q, prompt_k, prompt_v, suffix_q, suffix_k, suffix_v, prompt_of, suffix_len, out_weight
):
    info = jnp.stack([
        lax.axis_index("sample"), prompt_of[0], suffix_len[0], lax.axis_index("tensor")
    ]).astype(jnp.int32)

    both = jnp.concatenate([prompt_k, prompt_v], axis=1)
    other = swap(both, 2)
    blocks = gather_plane([
        both[None, :, :HD], both[None, :, HD:], other[None, :, :HD], other[None, :, HD:]])
    blocks = blocks + [swap(block, 1) for block in blocks]

    a_p = attend(True, info, prompt_q, prompt_k, prompt_v, blocks)
    p_1, p_3, p_2 = spread(a_p)
    a_s = attend(False, info, suffix_q, suffix_k, suffix_v, blocks)
    s_1, s_3, s_2 = spread(a_s)

    rows = jnp.stack([out_weight, swap(out_weight, 2)])
    weights = gather_plane([rows[None, :, :, i * 512:(i + 1) * 512] for i in range(4)])
    weights = weights + [swap(weight, 1) for weight in weights]

    total = project(0, False, info, a_p, a_s, weights, None)
    total = project(1, False, info, p_1, s_1, weights, total)
    total = project(3, False, info, p_3, s_3, weights, total)
    return tuple(project(2, True, info, p_2, s_2, weights, total))


def solution(mesh):
    both = P("sample", "tensor")
    return jax.shard_map(
        per_device,
        mesh=mesh,
        in_specs=(both,) * 6 + (P("sample"), P("sample"), both),
        out_specs=(both, both),
        check_vma=False,
    )
```

```python
import functools

import jax
import jax.numpy as jnp
from jax import lax
from jax.experimental import pallas as pl
from jax.experimental.pallas import tpu as pltpu
from jax.sharding import PartitionSpec as P

HD = 128
HEADS = 8
GROUP = 4
ROWS = 128
SCALE = HD ** (-0.5) * 1.4426950408889634
ORDERS = (((4, 12, 16, 48), (12, 4, 48, 16)), ((16, 48, 4, 12), (48, 16, 12, 4)))
VMEM = pl.BlockSpec(memory_space=pltpu.VMEM)
SMEM = pl.BlockSpec(memory_space=pltpu.SMEM)


def slot_table(me):
    there = jnp.arange(16, dtype=jnp.int32)
    apart = there ^ (me >> 2)
    low_x, high_x = apart & 1, (apart >> 1) & 1
    low_y, high_y = (apart >> 2) & 1, (apart >> 3) & 1
    used = {4: low_x ^ high_x, 12: high_x, 16: low_y ^ high_y, 48: high_y}
    rows = []
    for rc in range(2):
        for piece in range(2):
            first, second = [
                sum(used[mask] << step for step, mask in enumerate(order))
                for order in ORDERS[piece]]
            rows.append(jnp.where((me & 1) == rc, first, second))
    return jnp.concatenate(rows)


def slot_of(info, rc, piece, there):
    return info[4 + (rc * 2 + piece) * 16 + there]


def take(halves, slot):
    low = slot & 7
    return jnp.where(slot > 7, halves[1][low], halves[0][low])


def swap(x, masks):
    masks = masks if isinstance(masks, tuple) else (masks, masks)
    return lax.ppermute(x, "sample", [(s, s ^ masks[s & 1]) for s in range(64)])


def swap_tensor(x, masks):
    pairs = [(s * 4 + t, s * 4 + (t ^ masks[s & 1])) for s in range(64) for t in range(4)]
    return lax.ppermute(x, ("sample", "tensor"), pairs)


def after(x, *others):
    return lax.optimization_barrier((x, *others))[0]


def step_masks(piece, step):
    return (ORDERS[piece][0][step], ORDERS[piece][1][step])


def gather_step(pieces, step):
    return [swap(piece, step_masks(i, step)) for i, piece in enumerate(pieces)]


def join(pieces, came):
    return [jnp.concatenate([a, b], axis=0) for a, b in zip(pieces, came)]


def score_head(q, h, keys):
    return lax.dot_general(
        q[:, h * HD:(h + 1) * HD], keys, (((1,), (1,)), ((), ())),
        preferred_element_type=jnp.float32)


def add_values(acc, h, exps, shrink, values):
    acc[h] = acc[h] * jnp.concatenate([shrink, shrink], axis=1) + jnp.dot(
        exps, values, preferred_element_type=jnp.float32)


def attend_kernel(is_prompt, first, info, q, own_k, own_v, *refs):
    blocks, (out, top, acc) = refs[:8], refs[8:]
    me = info[0]
    core, low_z = me & 1, (me >> 1) & 1
    row = lax.broadcasted_iota(jnp.int32, (ROWS, ROWS), 0)
    col = lax.broadcasted_iota(jnp.int32, (ROWS, ROWS), 1)
    keys = own_k[...]
    values = jnp.concatenate([own_v[...], jnp.ones((ROWS, HD), jnp.bfloat16)], axis=1)
    scores = [
        jnp.where(row >= col, score_head(q, first + h, keys), -1e30) for h in range(GROUP)]
    best = [
        jnp.broadcast_to(jnp.max(part, axis=1, keepdims=True), (ROWS, HD)) for part in scores]
    exps = [
        jnp.exp2((part - high) * SCALE).astype(jnp.bfloat16) for part, high in zip(scores, best)]
    for h in range(GROUP):
        top[h] = best[h]
        acc[h] = jnp.dot(exps[h], values, preferred_element_type=jnp.float32)

    def absorb(pair, masked):
        begin = 8 * (me >> 5 if is_prompt else info[1]) + 2 * pair
        keys, values, allowed = [], [], []
        for there in (begin, begin + 1):
            for rc in range(2):
                for rz in range(2):
                    slot = slot_of(info, rc, rz, there)
                    both = take(blocks[rc * 4 + rz * 2:rc * 4 + rz * 2 + 2], slot)
                    keys.append(both[:, :HD])
                    values.append(both[:, HD:])
                    allowed.append(there * 4 + ((me ^ (rz * 2 + rc)) & 3) < me)
        keys = jnp.concatenate(keys, axis=0)
        values = jnp.concatenate(values, axis=0)
        values = jnp.concatenate([values, jnp.ones(values.shape, jnp.bfloat16)], axis=1)
        ahead = score_head(q, first, keys)
        behind = None
        for h in range(GROUP):
            scores = ahead
            if h + 1 < GROUP:
                ahead = score_head(q, first + h + 1, keys)
            parts = [scores[:, i * ROWS:(i + 1) * ROWS] for i in range(8)]
            if masked:
                parts = [jnp.where(ok, part, -1e30) for ok, part in zip(allowed, parts)]
            best = functools.reduce(jnp.maximum, parts)
            old = top[h]
            new = jnp.maximum(old, jnp.max(best, axis=1, keepdims=True))
            shrink = jnp.exp2((old - new) * SCALE)
            top[h] = new
            exps = jnp.concatenate(
                [jnp.exp2((part - new) * SCALE).astype(jnp.bfloat16) for part in parts], axis=1)
            if behind is not None:
                add_values(acc, h - 1, *behind, values)
            behind = exps, shrink
        add_values(acc, GROUP - 1, *behind, values)

    whole = (me & 31) >> 3 if is_prompt else 4
    lax.fori_loop(0, whole, lambda i, c: (absorb(i, False), c)[1], 0)
    if is_prompt:
        @pl.when((me & 7) > 0)
        def _():
            absorb(whole, True)
    for h in range(GROUP):
        result = acc[h][:, :HD] / acc[h][:, HD:]
        if not is_prompt:
            result = jnp.where(row < info[2], result, 0.0)
        result = jnp.where(core == 0, result, pltpu.roll(result, HD // 2, 1))
        place = pl.multiple_of((h ^ low_z) * HD, HD)
        out[:, pl.ds(place, HD)] = result.astype(jnp.bfloat16)


def attend(is_prompt, first, info, q, own_k, own_v, blocks):
    return pl.pallas_call(
        functools.partial(attend_kernel, is_prompt, first),
        out_shape=jax.ShapeDtypeStruct((ROWS, GROUP * HD), jnp.bfloat16),
        in_specs=[SMEM] + [VMEM] * (3 + len(blocks)),
        out_specs=VMEM,
        scratch_shapes=[
            pltpu.VMEM((GROUP, ROWS, HD), jnp.float32),
            pltpu.VMEM((GROUP, ROWS, 2 * HD), jnp.float32),
        ],
        compiler_params=pltpu.CompilerParams(vmem_limit_bytes=24 << 20),
        cost_estimate=pl.CostEstimate(
            flops=4 * GROUP * ROWS * 4224 * HD, transcendentals=GROUP * ROWS * 4224,
            bytes_accessed=4 << 20),
        name="attend_%s_%d" % ("prompt" if is_prompt else "suffix", first),
    )(info, q, own_k, own_v, *blocks)


def project_kernel(last, info, *refs):
    if last:
        heads, total_in, weights, (out_p, out_s) = refs[:4], refs[4], refs[5:13], refs[13:]
    else:
        heads, weights, total_out = refs[:8], refs[8:16], refs[16]
    core, tensor = info[0] & 1, info[3]
    near = jnp.where(core == 0, 1, 3)
    if last:
        pieces = [(tensor ^ near ^ 2, [ref[0] for ref in heads]),
                  (tensor ^ 2, [ref[1] for ref in heads])]
    else:
        pieces = [(tensor, [ref[...] for ref in heads[:4]]),
                  (tensor ^ near, [ref[...] for ref in heads[4:]])]
    for piece in range(2):
        lanes = slice(piece * 1024, (piece + 1) * 1024)
        total = total_in[:, lanes] if last else None
        for quarter, rows in pieces:
            rows = jnp.concatenate([
                jnp.concatenate(rows[:2], axis=1), jnp.concatenate(rows[2:], axis=1)], axis=0)
            held = []
            for x in range(4):
                there = quarter * 4 + x
                found = [
                    take(weights[rc * 4 + piece * 2:rc * 4 + piece * 2 + 2],
                         slot_of(info, rc, piece, there)) for rc in range(2)]
                for rz in range(2):
                    held += [found[0][rz], found[1][rz]]
            part = jnp.dot(
                rows, jnp.concatenate(held, axis=0), preferred_element_type=jnp.float32)
            total = part if total is None else total + part
        if last:
            out_p[:, lanes] = total[:ROWS].astype(jnp.bfloat16)
            out_s[:, lanes] = total[ROWS:].astype(jnp.bfloat16)
        else:
            total_out[:, lanes] = total


def project(last, info, heads, weights, total):
    if last:
        out_shape = [jax.ShapeDtypeStruct((ROWS, 2048), jnp.bfloat16)] * 2
    else:
        out_shape = jax.ShapeDtypeStruct((2 * ROWS, 2048), jnp.float32)
    args = [info, *heads] + ([total] if last else []) + list(weights)
    return pl.pallas_call(
        functools.partial(project_kernel, last),
        out_shape=out_shape,
        in_specs=[SMEM] + [VMEM] * (len(args) - 1),
        out_specs=[VMEM] * 2 if last else VMEM,
        compiler_params=pltpu.CompilerParams(vmem_limit_bytes=32 << 20),
        name="project_last" if last else "project_first",
    )(*args)


def per_device(
    prompt_q, prompt_k, prompt_v, suffix_q, suffix_k, suffix_v, prompt_of, suffix_len, out_weight
):
    me = lax.axis_index("sample").astype(jnp.int32)
    info = jnp.concatenate([
        jnp.stack([me, prompt_of[0], suffix_len[0], lax.axis_index("tensor").astype(jnp.int32)]),
        slot_table(me)])

    both = jnp.concatenate([prompt_k, prompt_v], axis=1)
    kv = [both[None], swap(both, 2)[None]]
    others = swap(out_weight, 2)
    kv = join(kv, gather_step(kv, 0))
    others = after(others, *kv)
    w = [jnp.stack([part[:, lanes] for part in (out_weight, others)])[None]
         for lanes in (slice(0, 1024), slice(1024, 2048))]
    w_came = gather_step(w, 0)
    kv = join(kv, gather_step(kv, 1))
    kv = join(kv, gather_step(kv, 2))
    w = join(w, [after(a, *kv) for a in w_came])
    came = gather_step([after(a, *w) for a in kv], 3)
    kv_mate = [swap(a, 1) for a in kv]
    w_came = gather_step([after(a, *came) for a in w], 1)
    came_mate = [swap(a, 1) for a in came]
    blocks = [kv[0], came[0], kv[1], came[1],
              kv_mate[0], came_mate[0], kv_mate[1], came_mate[1]]

    def attend_suffix(first, q):
        return attend(False, first, info, q, suffix_k, suffix_v, blocks)

    def attend_prompt(first, q):
        return attend(True, first, info, q, prompt_k, prompt_v, blocks)

    def to_near(a):
        return swap_tensor(a, (1, 3))

    def to_far(a, near):
        return swap_tensor(jnp.stack([a, near]), (3, 1))

    a0 = attend_suffix(0, suffix_q)
    a0, suffix_q, *w_came = lax.optimization_barrier((a0, suffix_q, *w_came))

    w = join(w, w_came)
    w_came = gather_step(w, 2)
    near0 = to_near(a0)
    a1 = attend_suffix(GROUP, suffix_q)
    a0, a1, near0, prompt_q = lax.optimization_barrier((a0, a1, near0, prompt_q))

    far0 = to_far(a0, near0)
    near1 = to_near(a1)
    a2 = attend_prompt(0, prompt_q)
    a1, a2, near1, far0, prompt_q, *w_came = lax.optimization_barrier(
        (a1, a2, near1, far0, prompt_q, *w_came))

    w = join(w, w_came)
    w_came = gather_step(w, 3)
    far1 = to_far(a1, near1)
    near2 = to_near(a2)
    a3 = attend_prompt(GROUP, prompt_q)
    a2, a3, near2, far1, *w_mate = lax.optimization_barrier((a2, a3, near2, far1, *w))

    far2 = to_far(a2, near2)
    near3 = to_near(a3)
    far3 = to_far(a3, near3)
    w_mate = [swap(after(a, near3), 1) for a in w_mate]
    w_came_mate = [swap(after(a, far2), 1) for a in w_came]
    weights = [w[0], w_came[0], w[1], w_came[1],
               w_mate[0], w_came_mate[0], w_mate[1], w_came_mate[1]]
    total = project(
        False, info, [a2, a3, a0, a1, near2, near3, near0, near1], weights, None)
    return tuple(project(True, info, [far2, far3, far0, far1], weights, total))


def solution(mesh):
    both = P("sample", "tensor")
    return jax.shard_map(
        per_device,
        mesh=mesh,
        in_specs=(both,) * 6 + (P("sample"), P("sample"), both),
        out_specs=(both, both),
        check_vma=False,
    )
```

```python
import functools

import jax
import jax.numpy as jnp
from jax import lax
from jax.experimental import pallas as pl
from jax.experimental.pallas import tpu as pltpu
from jax.sharding import PartitionSpec as P

HD = 128
HEADS = 8
ROWS = 128
SCALE = HD ** (-0.5) * 1.4426950408889634
ORDERS = (((4, 12, 16, 48), (12, 4, 48, 16)), ((16, 48, 4, 12), (48, 16, 12, 4)))
VMEM = pl.BlockSpec(memory_space=pltpu.VMEM)
SMEM = pl.BlockSpec(memory_space=pltpu.SMEM)


def slot_table(me):
    there = jnp.arange(16, dtype=jnp.int32)
    apart = there ^ (me >> 2)
    low_x, high_x = apart & 1, (apart >> 1) & 1
    low_y, high_y = (apart >> 2) & 1, (apart >> 3) & 1
    used = {4: low_x ^ high_x, 12: high_x, 16: low_y ^ high_y, 48: high_y}
    rows = []
    for rc in range(2):
        for piece in range(2):
            first, second = [
                sum(used[mask] << step for step, mask in enumerate(order))
                for order in ORDERS[piece]]
            rows.append(jnp.where((me & 1) == rc, first, second))
    return jnp.concatenate(rows)


def slot_of(info, rc, piece, there):
    return info[4 + (rc * 2 + piece) * 16 + there]


def take(halves, slot):
    low = slot & 7
    return jnp.where(slot > 7, halves[1][low], halves[0][low])


def swap(x, masks):
    masks = masks if isinstance(masks, tuple) else (masks, masks)
    return lax.ppermute(x, "sample", [(s, s ^ masks[s & 1]) for s in range(64)])


def swap_tensor(x, masks):
    pairs = [(s * 4 + t, s * 4 + (t ^ masks[s & 1])) for s in range(64) for t in range(4)]
    return lax.ppermute(x, ("sample", "tensor"), pairs)


def after(x, *others):
    return lax.optimization_barrier((x, *others))[0]


def step_masks(piece, step):
    return (ORDERS[piece][0][step], ORDERS[piece][1][step])


def gather_step(pieces, step):
    return [swap(piece, step_masks(i, step)) for i, piece in enumerate(pieces)]


def join(pieces, came):
    return [jnp.concatenate([a, b], axis=0) for a, b in zip(pieces, came)]


def score_head(q, h, keys):
    return lax.dot_general(
        q[:, h * HD:(h + 1) * HD], keys, (((1,), (1,)), ((), ())),
        preferred_element_type=jnp.float32)


def add_values(acc, h, exps, shrink, values):
    acc[h] = acc[h] * jnp.concatenate([shrink, shrink], axis=1) + jnp.dot(
        exps, values, preferred_element_type=jnp.float32)


def attend_kernel(is_prompt, first, count, info, q, own_k, own_v, *refs):
    blocks, (out, top, acc) = refs[:4], refs[4:]
    me = info[0]
    core, low_z = me & 1, (me >> 1) & 1
    row = lax.broadcasted_iota(jnp.int32, (ROWS, ROWS), 0)
    col = lax.broadcasted_iota(jnp.int32, (ROWS, ROWS), 1)
    keys = own_k[...]
    values = jnp.concatenate([own_v[...], jnp.ones((ROWS, HD), jnp.bfloat16)], axis=1)
    scores = [
        jnp.where(row >= col, score_head(q, first + h, keys), -1e30) for h in range(count)]
    best = [
        jnp.broadcast_to(jnp.max(part, axis=1, keepdims=True), (ROWS, HD)) for part in scores]
    exps = [
        jnp.exp2((part - high) * SCALE).astype(jnp.bfloat16) for part, high in zip(scores, best)]
    for h in range(count):
        top[h] = best[h]
        acc[h] = jnp.dot(exps[h], values, preferred_element_type=jnp.float32)

    def absorb(pair, masked):
        begin = 8 * (me >> 5 if is_prompt else info[1]) + 2 * pair
        keys, values, allowed = [], [], []
        for there in (begin, begin + 1):
            for rc in range(2):
                for rz in range(2):
                    slot = slot_of(info, rc, rz, there)
                    both = blocks[rc * 2 + rz][slot]
                    keys.append(both[:, :HD])
                    values.append(both[:, HD:])
                    allowed.append(there * 4 + ((me ^ (rz * 2 + rc)) & 3) < me)
        keys = jnp.concatenate(keys, axis=0)
        values = jnp.concatenate(values, axis=0)
        values = jnp.concatenate([values, jnp.ones(values.shape, jnp.bfloat16)], axis=1)
        ahead = score_head(q, first, keys)
        behind = None
        for h in range(count):
            scores = ahead
            if h + 1 < count:
                ahead = score_head(q, first + h + 1, keys)
            parts = [scores[:, i * ROWS:(i + 1) * ROWS] for i in range(8)]
            if masked:
                parts = [jnp.where(ok, part, -1e30) for ok, part in zip(allowed, parts)]
            best = functools.reduce(jnp.maximum, parts)
            old = top[h]
            new = jnp.maximum(old, jnp.max(best, axis=1, keepdims=True))
            shrink = jnp.exp2((old - new) * SCALE)
            top[h] = new
            exps = jnp.concatenate(
                [jnp.exp2((part - new) * SCALE).astype(jnp.bfloat16) for part in parts], axis=1)
            if behind is not None:
                add_values(acc, h - 1, *behind, values)
            behind = exps, shrink
        add_values(acc, count - 1, *behind, values)

    whole = (me & 31) >> 3 if is_prompt else 4
    lax.fori_loop(0, whole, lambda i, c: (absorb(i, False), c)[1], 0)
    if is_prompt:
        @pl.when((me & 7) > 0)
        def _():
            absorb(whole, True)
    for h in range(count):
        result = acc[h][:, :HD] / acc[h][:, HD:]
        if not is_prompt:
            result = jnp.where(row < info[2], result, 0.0)
        result = jnp.where(core == 0, result, pltpu.roll(result, HD // 2, 1))
        place = pl.multiple_of((h ^ low_z) * HD, HD)
        out[:, pl.ds(place, HD)] = result.astype(jnp.bfloat16)


def attend(is_prompt, first, count, info, q, own_k, own_v, blocks):
    return pl.pallas_call(
        functools.partial(attend_kernel, is_prompt, first, count),
        out_shape=jax.ShapeDtypeStruct((ROWS, count * HD), jnp.bfloat16),
        in_specs=[SMEM] + [VMEM] * (3 + len(blocks)),
        out_specs=VMEM,
        scratch_shapes=[
            pltpu.VMEM((count, ROWS, HD), jnp.float32),
            pltpu.VMEM((count, ROWS, 2 * HD), jnp.float32),
        ],
        compiler_params=pltpu.CompilerParams(vmem_limit_bytes=12 << 20),
        name="attend_%s_%d" % ("prompt" if is_prompt else "suffix", first),
    )(info, q, own_k, own_v, *blocks)


def project_kernel(kind, info, *refs):
    if kind == "first":
        heads, weights, (out,) = refs[:4], refs[4:12], refs[12:]
    else:
        heads, total, weights, (out,) = refs[0], refs[1], refs[2:10], refs[10:]
    core, tensor = info[0] & 1, info[3]
    near = jnp.where(core == 0, 1, 3)
    if kind == "first":
        pieces = [(tensor, jnp.concatenate([heads[0][...], heads[1][...]], axis=0)),
                  (tensor ^ near, jnp.concatenate([heads[2][...], heads[3][...]], axis=0))]
    else:
        pieces = [(tensor ^ near ^ 2, heads[0]), (tensor ^ 2, heads[1])]
    for piece in range(2):
        lanes = slice(piece * 1024, (piece + 1) * 1024)
        sums = None if kind == "first" else total[:, lanes]
        for quarter, rows in pieces:
            held = []
            for x in range(4):
                there = quarter * 4 + x
                found = [
                    take(weights[rc * 4 + piece * 2:rc * 4 + piece * 2 + 2],
                         slot_of(info, rc, piece, there)) for rc in range(2)]
                for rz in range(2):
                    held += [found[0][rz], found[1][rz]]
            part = jnp.dot(
                rows, jnp.concatenate(held, axis=0), preferred_element_type=jnp.float32)
            sums = part if sums is None else sums + part
        out[:, lanes] = sums.astype(out.dtype)


def project(kind, info, heads, weights, total=None):
    if kind == "first":
        out_shape = jax.ShapeDtypeStruct((2 * ROWS, 2048), jnp.float32)
    else:
        out_shape = jax.ShapeDtypeStruct((ROWS, 2048), jnp.bfloat16)
    args = [info, *heads] + ([] if kind == "first" else [total]) + list(weights)
    return pl.pallas_call(
        functools.partial(project_kernel, kind),
        out_shape=out_shape,
        in_specs=[SMEM] + [VMEM] * (len(args) - 1),
        out_specs=VMEM,
        compiler_params=pltpu.CompilerParams(vmem_limit_bytes=24 << 20),
        name="project_" + kind,
    )(*args)


def per_device(
    prompt_q, prompt_k, prompt_v, suffix_q, suffix_k, suffix_v, prompt_of, suffix_len, out_weight
):
    me = lax.axis_index("sample").astype(jnp.int32)
    info = jnp.concatenate([
        jnp.stack([me, prompt_of[0], suffix_len[0], lax.axis_index("tensor").astype(jnp.int32)]),
        slot_table(me)])

    other_k, other_v = swap(prompt_k, 2), swap(prompt_v, 2)
    kv = [jnp.concatenate([prompt_k, prompt_v], axis=1)[None],
          jnp.concatenate([other_k, other_v], axis=1)[None]]
    others = swap(after(out_weight, other_k), 2)
    kv = join(kv, gather_step(kv, 0))
    kv = join(kv, gather_step(kv, 1))
    others, info = lax.optimization_barrier((others, info))
    w = [jnp.stack([part[:, lanes] for part in (out_weight, others)])[None]
         for lanes in (slice(0, 1024), slice(1024, 2048))]
    w_came = gather_step(w, 0)
    kv = join(kv, gather_step([after(a, *w) for a in kv], 2))
    w = join(w, w_came)
    w_came = gather_step(w, 1)
    came = gather_step([after(a, *w) for a in kv], 3)
    kv_mate = [swap(a, 1) for a in kv]
    came_mate = [swap(a, 1) for a in came]
    blocks = [*join(kv, came), *join(kv_mate, came_mate)]
    w = join(w, [after(a, *came) for a in w_came])

    def to_near(a):
        return swap_tensor(a, (1, 3))

    def to_far(a):
        return swap_tensor(a, (3, 1))

    w_came = gather_step(w, 2)
    a_s = attend(False, 0, 8, info, after(suffix_q, *w), suffix_k, suffix_v, blocks)
    a_s, prompt_q, *w_came = lax.optimization_barrier((a_s, prompt_q, *w_came))

    w = join(w, w_came)
    w_came = gather_step(w, 3)
    near_s = to_near(a_s)
    a_p = attend(True, 0, 8, info, after(prompt_q, *w), prompt_k, prompt_v, blocks)
    a_s, near_s, a_p = lax.optimization_barrier((a_s, near_s, a_p))

    far_s = to_far(jnp.stack([a_s, near_s]))
    near_p = to_near(a_p)
    far_p = to_far(jnp.stack([a_p, near_p]))
    w_mate = [swap(after(a, a_p), 1) for a in w]
    w_came_mate = [swap(after(a, near_p), 1) for a in w_came]
    weights = [w[0], w_came[0], w[1], w_came[1],
               w_mate[0], w_came_mate[0], w_mate[1], w_came_mate[1]]
    total = project("first", info, [a_p, a_s, near_p, near_s], weights)
    out_s = project("rest", info, [far_s], weights, total[ROWS:])
    out_p = project("rest", info, [after(far_p, out_s)], weights, total[:ROWS])
    return out_p, out_s


def solution(mesh):
    both = P("sample", "tensor")
    return jax.shard_map(
        per_device,
        mesh=mesh,
        in_specs=(both,) * 6 + (P("sample"), P("sample"), both),
        out_specs=(both, both),
        check_vma=False,
    )
```

```python
import functools

import jax
import jax.numpy as jnp
from jax import lax
from jax.experimental import pallas as pl
from jax.experimental.pallas import tpu as pltpu
from jax.sharding import PartitionSpec as P

HD = 128
HEADS = 8
ROWS = 128
SCALE = HD ** (-0.5) * 1.4426950408889634
ORDERS = (((4, 12, 16, 48), (12, 4, 48, 16)), ((16, 48, 4, 12), (48, 16, 12, 4)))
VMEM = pl.BlockSpec(memory_space=pltpu.VMEM)
SMEM = pl.BlockSpec(memory_space=pltpu.SMEM)


def slot_table(me):
    there = jnp.arange(16, dtype=jnp.int32)
    apart = there ^ (me >> 2)
    low_x, high_x = apart & 1, (apart >> 1) & 1
    low_y, high_y = (apart >> 2) & 1, (apart >> 3) & 1
    used = {4: low_x ^ high_x, 12: high_x, 16: low_y ^ high_y, 48: high_y}
    rows = []
    for rc in range(2):
        for piece in range(2):
            first, second = [
                sum(used[mask] << step for step, mask in enumerate(order))
                for order in ORDERS[piece]]
            rows.append(jnp.where((me & 1) == rc, first, second))
    return jnp.concatenate(rows)


def slot_of(info, rc, piece, there):
    return info[4 + (rc * 2 + piece) * 16 + there]


def take(halves, slot):
    low = slot & 7
    return jnp.where(slot > 7, halves[1][low], halves[0][low])


def swap(x, masks):
    masks = masks if isinstance(masks, tuple) else (masks, masks)
    return lax.ppermute(x, "sample", [(s, s ^ masks[s & 1]) for s in range(64)])


def swap_tensor(x, masks):
    pairs = [(s * 4 + t, s * 4 + (t ^ masks[s & 1])) for s in range(64) for t in range(4)]
    return lax.ppermute(x, ("sample", "tensor"), pairs)


def after(x, *others):
    return lax.optimization_barrier((x, *others))[0]


def step_masks(piece, step):
    return (ORDERS[piece][0][step], ORDERS[piece][1][step])


def gather_step(pieces, step):
    return [swap(piece, step_masks(i, step)) for i, piece in enumerate(pieces)]


def join(pieces, came):
    return [jnp.concatenate([a, b], axis=0) for a, b in zip(pieces, came)]


def score_head(q, h, keys):
    return lax.dot_general(
        q[:, h * HD:(h + 1) * HD], keys, (((1,), (1,)), ((), ())),
        preferred_element_type=jnp.float32)


def add_values(acc, h, exps, shrink, values):
    acc[h] = acc[h] * jnp.concatenate([shrink, shrink], axis=1) + jnp.dot(
        exps, values, preferred_element_type=jnp.float32)


def attend_kernel(is_prompt, first, count, info, q, own_k, own_v, *refs):
    blocks, (out, top, acc) = refs[:4], refs[4:]
    me = info[0]
    core, low_z = me & 1, (me >> 1) & 1
    row = lax.broadcasted_iota(jnp.int32, (ROWS, ROWS), 0)
    col = lax.broadcasted_iota(jnp.int32, (ROWS, ROWS), 1)
    keys = own_k[...]
    values = jnp.concatenate([own_v[...], jnp.ones((ROWS, HD), jnp.bfloat16)], axis=1)
    scores = [
        jnp.where(row >= col, score_head(q, first + h, keys), -1e30) for h in range(count)]
    best = [
        jnp.broadcast_to(jnp.max(part, axis=1, keepdims=True), (ROWS, HD)) for part in scores]
    exps = [
        jnp.exp2((part - high) * SCALE).astype(jnp.bfloat16) for part, high in zip(scores, best)]
    for h in range(count):
        top[h] = best[h]
        acc[h] = jnp.dot(exps[h], values, preferred_element_type=jnp.float32)

    def absorb(pair, masked):
        begin = 8 * (me >> 5 if is_prompt else info[1]) + 2 * pair
        keys, values, allowed = [], [], []
        for there in (begin, begin + 1):
            for rc in range(2):
                for rz in range(2):
                    slot = slot_of(info, rc, rz, there)
                    both = blocks[rc * 2 + rz][slot]
                    keys.append(both[:, :HD])
                    values.append(both[:, HD:])
                    allowed.append(there * 4 + ((me ^ (rz * 2 + rc)) & 3) < me)
        keys = jnp.concatenate(keys, axis=0)
        values = jnp.concatenate(values, axis=0)
        values = jnp.concatenate([values, jnp.ones(values.shape, jnp.bfloat16)], axis=1)
        ahead = score_head(q, first, keys)
        behind = None
        for h in range(count):
            scores = ahead
            if h + 1 < count:
                ahead = score_head(q, first + h + 1, keys)
            parts = [scores[:, i * ROWS:(i + 1) * ROWS] for i in range(8)]
            if masked:
                parts = [jnp.where(ok, part, -1e30) for ok, part in zip(allowed, parts)]
            best = functools.reduce(jnp.maximum, parts)
            old = top[h]
            new = jnp.maximum(old, jnp.max(best, axis=1, keepdims=True))
            shrink = jnp.exp2((old - new) * SCALE)
            top[h] = new
            exps = jnp.concatenate(
                [jnp.exp2((part - new) * SCALE).astype(jnp.bfloat16) for part in parts], axis=1)
            if behind is not None:
                add_values(acc, h - 1, *behind, values)
            behind = exps, shrink
        add_values(acc, count - 1, *behind, values)

    whole = (me & 31) >> 3 if is_prompt else 4
    lax.fori_loop(0, whole, lambda i, c: (absorb(i, False), c)[1], 0)
    if is_prompt:
        @pl.when((me & 7) > 0)
        def _():
            absorb(whole, True)
    for h in range(count):
        result = acc[h][:, :HD] / acc[h][:, HD:]
        if not is_prompt:
            result = jnp.where(row < info[2], result, 0.0)
        result = jnp.where(core == 0, result, pltpu.roll(result, HD // 2, 1))
        place = pl.multiple_of((h ^ low_z) * HD, HD)
        out[:, pl.ds(place, HD)] = result.astype(jnp.bfloat16)


def attend(is_prompt, first, count, info, q, own_k, own_v, blocks):
    return pl.pallas_call(
        functools.partial(attend_kernel, is_prompt, first, count),
        out_shape=jax.ShapeDtypeStruct((ROWS, count * HD), jnp.bfloat16),
        in_specs=[SMEM] + [VMEM] * (3 + len(blocks)),
        out_specs=VMEM,
        scratch_shapes=[
            pltpu.VMEM((count, ROWS, HD), jnp.float32),
            pltpu.VMEM((count, ROWS, 2 * HD), jnp.float32),
        ],
        compiler_params=pltpu.CompilerParams(vmem_limit_bytes=12 << 20),
        name="attend_%s_%d" % ("prompt" if is_prompt else "suffix", first),
    )(info, q, own_k, own_v, *blocks)


def project_kernel(info, a_p, a_s, near_s, mixed, far_p, *refs):
    weights, (out_p, out_s) = refs[:8], refs[8:]
    core, tensor = info[0] & 1, info[3]
    near = jnp.where(core == 0, 1, 3)
    pieces = [
        (quarter, jnp.concatenate(rows, axis=0)) for quarter, rows in (
            (tensor, (a_p[...], a_s[...])),
            (tensor ^ near, (far_p[0], near_s[...])),
            (tensor ^ near ^ 2, (mixed[2], mixed[0])),
            (tensor ^ 2, (far_p[1], mixed[1])))]
    for piece in range(2):
        lanes = slice(piece * 1024, (piece + 1) * 1024)
        sums = None
        for quarter, rows in pieces:
            held = []
            for x in range(4):
                there = quarter * 4 + x
                found = [
                    take(weights[rc * 4 + piece * 2:rc * 4 + piece * 2 + 2],
                         slot_of(info, rc, piece, there)) for rc in range(2)]
                for rz in range(2):
                    held += [found[0][rz], found[1][rz]]
            part = jnp.dot(
                rows, jnp.concatenate(held, axis=0), preferred_element_type=jnp.float32)
            sums = part if sums is None else sums + part
        out_p[:, lanes] = sums[:ROWS].astype(jnp.bfloat16)
        out_s[:, lanes] = sums[ROWS:].astype(jnp.bfloat16)


def project(info, heads, weights):
    args = [info, *heads, *weights]
    return pl.pallas_call(
        project_kernel,
        out_shape=[jax.ShapeDtypeStruct((ROWS, 2048), jnp.bfloat16)] * 2,
        in_specs=[SMEM] + [VMEM] * (len(args) - 1),
        out_specs=[VMEM] * 2,
        compiler_params=pltpu.CompilerParams(vmem_limit_bytes=24 << 20),
        name="project",
    )(*args)


def per_device(
    prompt_q, prompt_k, prompt_v, suffix_q, suffix_k, suffix_v, prompt_of, suffix_len, out_weight
):
    me = lax.axis_index("sample").astype(jnp.int32)
    info = jnp.concatenate([
        jnp.stack([me, prompt_of[0], suffix_len[0], lax.axis_index("tensor").astype(jnp.int32)]),
        slot_table(me)])

    other_k, other_v = swap(prompt_k, 2), swap(prompt_v, 2)
    own = lax.optimization_barrier(jnp.concatenate([prompt_k, prompt_v], axis=1))
    kv = [own[None], jnp.concatenate([other_k, other_v], axis=1)[None]]
    others = swap(after(out_weight, other_k), 2)
    kv = join(kv, gather_step(kv, 0))
    kv = join(kv, gather_step(kv, 1))
    others, info, out_weight, _ = lax.optimization_barrier((others, info, out_weight, kv[0]))
    w = [jnp.stack([part[:, lanes] for part in (out_weight, others)])[None]
         for lanes in (slice(0, 1024), slice(1024, 2048))]
    w_came = gather_step(w, 0)
    kv = join(kv, gather_step([after(a, *w) for a in kv], 2))
    w = join(w, w_came)
    w_came = gather_step(w, 1)
    came = gather_step([after(a, *w) for a in kv], 3)
    kv_mate = [swap(a, 1) for a in kv]
    came_mate = [swap(a, 1) for a in came]
    blocks = [*join(kv, came), *join(kv_mate, came_mate)]

    a_s = attend(False, 0, 8, info, suffix_q, suffix_k, suffix_v, blocks)
    a_s, prompt_q, *w_came = lax.optimization_barrier((a_s, prompt_q, *w_came))

    w = join(w, w_came)
    w_3 = gather_step(w, 2)
    near_s = swap_tensor(a_s, (1, 3))
    a_p = attend(True, 0, 8, info, after(prompt_q, *w), prompt_k, prompt_v, blocks)
    a_s, near_s, a_p, *w = lax.optimization_barrier((a_s, near_s, a_p, *w))

    mixed = swap_tensor(jnp.stack([a_s, near_s, a_p]), (3, 1))
    w_4 = gather_step(w, 3)
    mixed, *w = lax.optimization_barrier((mixed, *w, *w_3, *w_4))
    w, w_3, w_4 = w[:2], w[2:4], w[4:]

    far_p = swap_tensor(jnp.stack([a_p, mixed[2]]), (1, 3))
    w_5 = gather_step(w_3, 3)
    w = join(w, w_3)
    w_mate = [swap(a, 1) for a in w]
    far_p, *w_mate = lax.optimization_barrier((far_p, *w_mate))

    *w_5, _ = lax.optimization_barrier((*w_5, far_p))
    w_5_mate = [swap(a, 1) for a in w_5]
    w_4_mate = [swap(after(a, *w_5), 1) for a in w_4]
    w_came = join(w_4, w_5)
    w_came_mate = join(w_4_mate, w_5_mate)
    weights = [w[0], w_came[0], w[1], w_came[1],
               w_mate[0], w_came_mate[0], w_mate[1], w_came_mate[1]]
    return tuple(project(info, [a_p, a_s, near_s, mixed, far_p], weights))


def solution(mesh):
    both = P("sample", "tensor")
    return jax.shard_map(
        per_device,
        mesh=mesh,
        in_specs=(both,) * 6 + (P("sample"), P("sample"), both),
        out_specs=(both, both),
        check_vma=False,
    )
```

```python
import functools

import jax
import jax.numpy as jnp
from jax import lax
from jax.experimental import pallas as pl
from jax.experimental.pallas import tpu as pltpu
from jax.sharding import PartitionSpec as P

HD = 128
HEADS = 8
ROWS = 128
SCALE = HD ** (-0.5) * 1.4426950408889634
ORDERS = (((4, 12, 16, 48), (12, 4, 48, 16)), ((16, 48, 4, 12), (48, 16, 12, 4)))
VMEM = pl.BlockSpec(memory_space=pltpu.VMEM)
SMEM = pl.BlockSpec(memory_space=pltpu.SMEM)


def slot_table(me):
    there = jnp.arange(16, dtype=jnp.int32)
    apart = there ^ (me >> 2)
    low_x, high_x = apart & 1, (apart >> 1) & 1
    low_y, high_y = (apart >> 2) & 1, (apart >> 3) & 1
    used = {4: low_x ^ high_x, 12: high_x, 16: low_y ^ high_y, 48: high_y}
    rows = []
    for rc in range(2):
        for piece in range(2):
            first, second = [
                sum(used[mask] << step for step, mask in enumerate(order))
                for order in ORDERS[piece]]
            rows.append(jnp.where((me & 1) == rc, first, second))
    return jnp.concatenate(rows)


def slot_of(info, rc, piece, there):
    return info[4 + (rc * 2 + piece) * 16 + there]


def take(halves, slot):
    low = slot & 7
    return jnp.where(slot > 7, halves[1][low], halves[0][low])


def swap(x, masks):
    masks = masks if isinstance(masks, tuple) else (masks, masks)
    return lax.ppermute(x, "sample", [(s, s ^ masks[s & 1]) for s in range(64)])


def swap_tensor(x, masks):
    pairs = [(s * 4 + t, s * 4 + (t ^ masks[s & 1])) for s in range(64) for t in range(4)]
    return lax.ppermute(x, ("sample", "tensor"), pairs)


def after(x, *others):
    return lax.optimization_barrier((x, *others))[0]


def step_masks(piece, step):
    return (ORDERS[piece][0][step], ORDERS[piece][1][step])


def gather_step(pieces, step):
    return [swap(piece, step_masks(i, step)) for i, piece in enumerate(pieces)]


def join(pieces, came):
    return [jnp.concatenate([a, b], axis=0) for a, b in zip(pieces, came)]


def score_head(q, h, keys):
    return lax.dot_general(
        q[:, h * HD:(h + 1) * HD], keys, (((1,), (1,)), ((), ())),
        preferred_element_type=jnp.float32)


def add_values(acc, h, exps, shrink, values):
    fresh = jnp.dot(exps, values, preferred_element_type=jnp.float32)
    if shrink is not None:
        fresh = acc[h] * jnp.concatenate([shrink, shrink], axis=1) + fresh
    acc[h] = fresh


def attend_kernel(is_prompt, first, count, info, q, own_k, own_v, *refs):
    blocks, (out, top, acc) = refs[:4], refs[4:]
    me = info[0]
    row = lax.broadcasted_iota(jnp.int32, (ROWS, ROWS), 0)
    ahead_by = row - lax.broadcasted_iota(jnp.int32, (ROWS, ROWS), 1)

    def absorb(pair, opening):
        begin = 8 * (me >> 5 if is_prompt else info[1]) + 2 * pair
        keys, values, floors = [], [], []
        for there in (begin, begin + 1):
            for rc in range(2):
                for rz in range(2):
                    both = blocks[rc * 2 + rz][slot_of(info, rc, rz, there)]
                    keys.append(both[:, :HD])
                    values.append(both[:, HD:])
                    later = there * 4 + ((me ^ (rz * 2 + rc)) & 3) - me
                    floors.append(later * ROWS if is_prompt and opening else None)
        if opening and not is_prompt:
            keys.append(own_k[...])
            values.append(own_v[...])
            floors.append(0)
        keys = jnp.concatenate(keys, axis=0)
        values = jnp.concatenate(values, axis=0)
        values = jnp.concatenate([values, jnp.ones(values.shape, jnp.bfloat16)], axis=1)
        ready = [score_head(q, first, keys), score_head(q, first + 1, keys)]
        behind = None
        for h in range(count):
            scores = ready.pop(0)
            if h + 2 < count:
                ready.append(score_head(q, first + h + 2, keys))
            parts = [scores[:, i * ROWS:(i + 1) * ROWS] for i in range(len(floors))]
            parts = [
                part if floor is None else jnp.where(ahead_by >= floor, part, -1e30)
                for floor, part in zip(floors, parts)]
            new = jnp.max(functools.reduce(jnp.maximum, parts), axis=1, keepdims=True)
            if opening:
                new = jnp.broadcast_to(new, (ROWS, HD))
                shrink = None
            else:
                old = top[h]
                new = jnp.maximum(old, new)
                shrink = jnp.exp2((old - new) * SCALE)
            top[h] = new
            exps = jnp.concatenate(
                [jnp.exp2((part - new) * SCALE).astype(jnp.bfloat16) for part in parts], axis=1)
            if behind is not None:
                add_values(acc, h - 1, *behind, values)
            behind = exps, shrink
        add_values(acc, count - 1, *behind, values)

    if is_prompt:
        last = (me & 31) >> 3
        absorb(last, True)
        lax.fori_loop(0, last, lambda i, c: (absorb(i, False), c)[1], 0)
    else:
        for i in range(4):
            absorb(i, i == 0)
    core, low_z = me & 1, (me >> 1) & 1
    for h in range(count):
        result = acc[h][:, :HD] / acc[h][:, HD:]
        if not is_prompt:
            result = jnp.where(row < info[2], result, 0.0)
        result = jnp.where(core == 0, result, pltpu.roll(result, HD // 2, 1))
        place = pl.multiple_of((h ^ low_z) * HD, HD)
        out[:, pl.ds(place, HD)] = result.astype(jnp.bfloat16)


def attend(is_prompt, first, count, info, q, own_k, own_v, blocks):
    return pl.pallas_call(
        functools.partial(attend_kernel, is_prompt, first, count),
        out_shape=jax.ShapeDtypeStruct((ROWS, count * HD), jnp.bfloat16),
        in_specs=[SMEM] + [VMEM] * (3 + len(blocks)),
        out_specs=VMEM,
        scratch_shapes=[
            pltpu.VMEM((count, ROWS, HD), jnp.float32),
            pltpu.VMEM((count, ROWS, 2 * HD), jnp.float32),
        ],
        compiler_params=pltpu.CompilerParams(vmem_limit_bytes=12 << 20),
        name="attend_%s_%d" % ("prompt" if is_prompt else "suffix", first),
    )(info, q, own_k, own_v, *blocks)


def project_kernel(info, a_p, a_s, near_s, mixed, far_p, *refs):
    weights, (out_p, out_s) = refs[:8], refs[8:]
    core, tensor = info[0] & 1, info[3]
    near = jnp.where(core == 0, 1, 3)
    pieces = [
        (quarter, jnp.concatenate(rows, axis=0)) for quarter, rows in (
            (tensor, (a_p[...], a_s[...])),
            (tensor ^ near, (far_p[0], near_s[...])),
            (tensor ^ near ^ 2, (mixed[2], mixed[0])),
            (tensor ^ 2, (far_p[1], mixed[1])))]
    for piece in range(2):
        lanes = slice(piece * 1024, (piece + 1) * 1024)
        sums = None
        for quarter, rows in pieces:
            held = []
            for x in range(4):
                there = quarter * 4 + x
                found = [
                    take(weights[rc * 4 + piece * 2:rc * 4 + piece * 2 + 2],
                         slot_of(info, rc, piece, there)) for rc in range(2)]
                for rz in range(2):
                    held += [found[0][rz], found[1][rz]]
            part = jnp.dot(
                rows, jnp.concatenate(held, axis=0), preferred_element_type=jnp.float32)
            sums = part if sums is None else sums + part
        out_p[:, lanes] = sums[:ROWS].astype(jnp.bfloat16)
        out_s[:, lanes] = sums[ROWS:].astype(jnp.bfloat16)


def project(info, heads, weights):
    args = [info, *heads, *weights]
    return pl.pallas_call(
        project_kernel,
        out_shape=[jax.ShapeDtypeStruct((ROWS, 2048), jnp.bfloat16)] * 2,
        in_specs=[SMEM] + [VMEM] * (len(args) - 1),
        out_specs=[VMEM] * 2,
        compiler_params=pltpu.CompilerParams(vmem_limit_bytes=24 << 20),
        name="project",
    )(*args)


def per_device(
    prompt_q, prompt_k, prompt_v, suffix_q, suffix_k, suffix_v, prompt_of, suffix_len, out_weight
):
    me = lax.axis_index("sample").astype(jnp.int32)
    info = jnp.concatenate([
        jnp.stack([me, prompt_of[0], suffix_len[0], lax.axis_index("tensor").astype(jnp.int32)]),
        slot_table(me)])

    other_k, other_v = swap(prompt_k, 2), swap(prompt_v, 2)
    own = lax.optimization_barrier(jnp.concatenate([prompt_k, prompt_v], axis=1))
    kv = [own[None], jnp.concatenate([other_k, other_v], axis=1)[None]]
    others = swap(after(out_weight, other_k), 2)
    kv = join(kv, gather_step(kv, 0))
    kv = join(kv, gather_step(kv, 1))
    others, info, out_weight, _ = lax.optimization_barrier((others, info, out_weight, kv[0]))
    w = [jnp.stack([part[:, lanes] for part in (out_weight, others)])[None]
         for lanes in (slice(0, 1024), slice(1024, 2048))]
    w_came = gather_step(w, 0)
    kv = join(kv, gather_step([after(a, *w) for a in kv], 2))
    w = join(w, w_came)
    w_came = gather_step(w, 1)
    came = gather_step([after(a, *w) for a in kv], 3)
    kv_mate = [swap(a, 1) for a in kv]
    came_mate = [swap(a, 1) for a in came]
    blocks = [*join(kv, came), *join(kv_mate, came_mate)]

    a_s = attend(False, 0, 8, info, suffix_q, suffix_k, suffix_v, blocks)
    a_s, prompt_q, *w_came = lax.optimization_barrier((a_s, prompt_q, *w_came))

    w = join(w, w_came)
    w_3 = gather_step(w, 2)
    near_s = swap_tensor(a_s, (1, 3))
    a_p = attend(True, 0, 8, info, after(prompt_q, *w), prompt_k, prompt_v, blocks)
    a_s, near_s, a_p = lax.optimization_barrier((a_s, near_s, a_p))
    w = join(w, [after(a, a_p) for a in w_3])

    mixed = swap_tensor(jnp.stack([a_s, near_s, a_p]), (3, 1))
    w_came = gather_step(w, 3)
    far_p = swap_tensor(jnp.stack([a_p, mixed[2]]), (1, 3))
    w_mate = [swap(a, 1) for a in w]
    w_came = [after(a, mixed) for a in w_came]
    w_came_mate = [swap(a, 1) for a in w_came]
    weights = [w[0], w_came[0], w[1], w_came[1],
               w_mate[0], w_came_mate[0], w_mate[1], w_came_mate[1]]
    return tuple(project(info, [a_p, a_s, near_s, mixed, far_p], weights))


def solution(mesh):
    both = P("sample", "tensor")
    return jax.shard_map(
        per_device,
        mesh=mesh,
        in_specs=(both,) * 6 + (P("sample"), P("sample"), both),
        out_specs=(both, both),
        check_vma=False,
    )
```

```python
import functools

import jax
import jax.numpy as jnp
from jax import lax
from jax.experimental import pallas as pl
from jax.experimental.pallas import tpu as pltpu
from jax.sharding import PartitionSpec as P

HD = 128
HEADS = 8
ROWS = 128
SCALE = HD ** (-0.5) * 1.4426950408889634
ORDERS = (((4, 12, 16, 48), (12, 4, 48, 16)), ((16, 48, 4, 12), (48, 16, 12, 4)))
VMEM = pl.BlockSpec(memory_space=pltpu.VMEM)
SMEM = pl.BlockSpec(memory_space=pltpu.SMEM)


def slot_table(me):
    there = jnp.arange(16, dtype=jnp.int32)
    apart = there ^ (me >> 2)
    low_x, high_x = apart & 1, (apart >> 1) & 1
    low_y, high_y = (apart >> 2) & 1, (apart >> 3) & 1
    used = {4: low_x ^ high_x, 12: high_x, 16: low_y ^ high_y, 48: high_y}
    rows = []
    for rc in range(2):
        for piece in range(2):
            first, second = [
                sum(used[mask] << step for step, mask in enumerate(order))
                for order in ORDERS[piece]]
            rows.append(jnp.where((me & 1) == rc, first, second))
    return jnp.concatenate(rows)


def slot_of(info, rc, piece, there):
    return info[4 + (rc * 2 + piece) * 16 + there]


def take(halves, slot):
    low = slot & 7
    return jnp.where(slot > 7, halves[1][low], halves[0][low])


def swap(x, masks):
    masks = masks if isinstance(masks, tuple) else (masks, masks)
    return lax.ppermute(x, "sample", [(s, s ^ masks[s & 1]) for s in range(64)])


def swap_tensor(x, masks):
    pairs = [(s * 4 + t, s * 4 + (t ^ masks[s & 1])) for s in range(64) for t in range(4)]
    return lax.ppermute(x, ("sample", "tensor"), pairs)


def after(x, *others):
    return lax.optimization_barrier((x, *others))[0]


def step_masks(piece, step):
    return (ORDERS[piece][0][step], ORDERS[piece][1][step])


def gather_step(pieces, step):
    return [swap(piece, step_masks(i, step)) for i, piece in enumerate(pieces)]


def join(pieces, came):
    return [jnp.concatenate([a, b], axis=0) for a, b in zip(pieces, came)]


def score_head(q, h, keys):
    return lax.dot_general(
        q[:, h * HD:(h + 1) * HD], keys, (((1,), (1,)), ((), ())),
        preferred_element_type=jnp.float32)


def add_values(acc, h, exps, shrink, values):
    fresh = jnp.dot(exps, values, preferred_element_type=jnp.float32)
    if shrink is not None:
        fresh = acc[h] * jnp.concatenate([shrink, shrink], axis=1) + fresh
    acc[h] = fresh


def attend_kernel(is_prompt, first, count, info, q, own_k, own_v, *refs):
    blocks, (out, top, acc) = refs[:4], refs[4:]
    me = info[0]
    row = lax.broadcasted_iota(jnp.int32, (ROWS, ROWS), 0)
    ahead_by = row - lax.broadcasted_iota(jnp.int32, (ROWS, ROWS), 1)

    def absorb(pair, opening):
        begin = 8 * (me >> 5 if is_prompt else info[1]) + 2 * pair
        keys, values, floors = [], [], []
        for there in (begin, begin + 1):
            for rc in range(2):
                for rz in range(2):
                    both = blocks[rc * 2 + rz][slot_of(info, rc, rz, there)]
                    keys.append(both[:, :HD])
                    values.append(both[:, HD:])
                    later = there * 4 + ((me ^ (rz * 2 + rc)) & 3) - me
                    floors.append(later * ROWS if is_prompt and opening else None)
        if opening and not is_prompt:
            keys.append(own_k[...])
            values.append(own_v[...])
            floors.append(0)
        keys = jnp.concatenate(keys, axis=0)
        values = jnp.concatenate(values, axis=0)
        values = jnp.concatenate([values, jnp.ones(values.shape, jnp.bfloat16)], axis=1)
        ready = [score_head(q, first, keys), score_head(q, first + 1, keys)]
        behind = None
        for h in range(count):
            scores = ready.pop(0)
            if h + 2 < count:
                ready.append(score_head(q, first + h + 2, keys))
            parts = [scores[:, i * ROWS:(i + 1) * ROWS] for i in range(len(floors))]
            parts = [
                part if floor is None else jnp.where(ahead_by >= floor, part, -1e30)
                for floor, part in zip(floors, parts)]
            new = jnp.max(functools.reduce(jnp.maximum, parts), axis=1, keepdims=True)
            if opening:
                new = jnp.broadcast_to(new, (ROWS, HD))
                shrink = None
            else:
                old = top[h]
                new = jnp.maximum(old, new)
                shrink = jnp.exp2((old - new) * SCALE)
            top[h] = new
            exps = jnp.concatenate(
                [jnp.exp2((part - new) * SCALE).astype(jnp.bfloat16) for part in parts], axis=1)
            if behind is not None:
                add_values(acc, h - 1, *behind, values)
            behind = exps, shrink
        add_values(acc, count - 1, *behind, values)

    if is_prompt:
        last = (me & 31) >> 3
        absorb(last, True)
        lax.fori_loop(0, last, lambda i, c: (absorb(i, False), c)[1], 0)
    else:
        for i in range(4):
            absorb(i, i == 0)
    core, low_z = me & 1, (me >> 1) & 1
    for h in range(count):
        result = acc[h][:, :HD] / acc[h][:, HD:]
        if not is_prompt:
            result = jnp.where(row < info[2], result, 0.0)
        result = jnp.where(core == 0, result, pltpu.roll(result, HD // 2, 1))
        place = pl.multiple_of((h ^ low_z) * HD, HD)
        out[:, pl.ds(place, HD)] = result.astype(jnp.bfloat16)


def attend(is_prompt, first, count, info, q, own_k, own_v, blocks):
    return pl.pallas_call(
        functools.partial(attend_kernel, is_prompt, first, count),
        out_shape=jax.ShapeDtypeStruct((ROWS, count * HD), jnp.bfloat16),
        in_specs=[SMEM] + [VMEM] * (3 + len(blocks)),
        out_specs=VMEM,
        scratch_shapes=[
            pltpu.VMEM((count, ROWS, HD), jnp.float32),
            pltpu.VMEM((count, ROWS, 2 * HD), jnp.float32),
        ],
        compiler_params=pltpu.CompilerParams(vmem_limit_bytes=12 << 20),
        name="attend_%s_%d" % ("prompt" if is_prompt else "suffix", first),
    )(info, q, own_k, own_v, *blocks)


def project_kernel(info, a_p, a_s, near_s, mixed, far_p, *refs):
    weights, (out_p, out_s) = refs[:8], refs[8:]
    core, tensor = info[0] & 1, info[3]
    near = jnp.where(core == 0, 1, 3)
    pieces = [
        (quarter, jnp.concatenate(rows, axis=0)) for quarter, rows in (
            (tensor, (a_p[...], a_s[...])),
            (tensor ^ near, (far_p[0], near_s[...])),
            (tensor ^ near ^ 2, (mixed[2], mixed[0])),
            (tensor ^ 2, (far_p[1], mixed[1])))]
    for piece in range(2):
        lanes = slice(piece * 1024, (piece + 1) * 1024)
        sums = None
        for quarter, rows in pieces:
            held = []
            for x in range(4):
                there = quarter * 4 + x
                found = [
                    take(weights[rc * 4 + piece * 2:rc * 4 + piece * 2 + 2],
                         slot_of(info, rc, piece, there)) for rc in range(2)]
                for rz in range(2):
                    held += [found[0][rz], found[1][rz]]
            part = jnp.dot(
                rows, jnp.concatenate(held, axis=0), preferred_element_type=jnp.float32)
            sums = part if sums is None else sums + part
        out_p[:, lanes] = sums[:ROWS].astype(jnp.bfloat16)
        out_s[:, lanes] = sums[ROWS:].astype(jnp.bfloat16)


def project(info, heads, weights):
    args = [info, *heads, *weights]
    return pl.pallas_call(
        project_kernel,
        out_shape=[jax.ShapeDtypeStruct((ROWS, 2048), jnp.bfloat16)] * 2,
        in_specs=[SMEM] + [VMEM] * (len(args) - 1),
        out_specs=[VMEM] * 2,
        compiler_params=pltpu.CompilerParams(vmem_limit_bytes=24 << 20),
        name="project",
    )(*args)


def per_device(
    prompt_q, prompt_k, prompt_v, suffix_q, suffix_k, suffix_v, prompt_of, suffix_len, out_weight
):
    me = lax.axis_index("sample").astype(jnp.int32)
    info = jnp.concatenate([
        jnp.stack([me, prompt_of[0], suffix_len[0], lax.axis_index("tensor").astype(jnp.int32)]),
        slot_table(me)])

    other_k, other_v = swap(prompt_k, 2), swap(prompt_v, 2)
    own = lax.optimization_barrier(jnp.concatenate([prompt_k, prompt_v], axis=1))
    kv = [own[None], jnp.concatenate([other_k, other_v], axis=1)[None]]
    others = swap(after(out_weight, other_k), 2)
    kv = join(kv, gather_step(kv, 0))
    kv = join(kv, gather_step(kv, 1))
    others, info, out_weight, _ = lax.optimization_barrier((others, info, out_weight, kv[0]))
    w = [jnp.stack([part[:, lanes] for part in (out_weight, others)])[None]
         for lanes in (slice(0, 1024), slice(1024, 2048))]
    w_came = gather_step(w, 0)
    kv = join(kv, gather_step([after(a, *w) for a in kv], 2))
    w = join(w, w_came)
    w_came = gather_step(w, 1)
    came = gather_step(kv, 3)
    kv_mate = [swap(a, 1) for a in kv]
    came_mate = [swap(a, 1) for a in came]
    blocks = [*join(kv, came), *join(kv_mate, came_mate)]

    a_s = attend(False, 0, 8, info, suffix_q, suffix_k, suffix_v, blocks)
    a_s, prompt_q, *w_came = lax.optimization_barrier((a_s, prompt_q, *w_came))

    w = join(w, w_came)
    w_3 = gather_step(w, 2)
    near_s = swap_tensor(a_s, (1, 3))
    a_p = attend(True, 0, 8, info, after(prompt_q, *w), prompt_k, prompt_v, blocks)
    a_s, near_s, a_p = lax.optimization_barrier((a_s, near_s, a_p))
    mixed = swap_tensor(jnp.stack([a_s, near_s, a_p]), (3, 1))
    w = join(w, [after(a, a_p) for a in w_3])
    w_came = gather_step(w, 3)
    far_p = swap_tensor(jnp.stack([a_p, mixed[2]]), (1, 3))
    w_mate = [swap(a, 1) for a in w]
    w_came = [after(a, mixed) for a in w_came]
    w_came_mate = [swap(w_came[0], 1), swap(after(w_came[1], far_p), 1)]
    weights = [w[0], w_came[0], w[1], w_came[1],
               w_mate[0], w_came_mate[0], w_mate[1], w_came_mate[1]]
    return tuple(project(info, [a_p, a_s, near_s, mixed, far_p], weights))


def solution(mesh):
    both = P("sample", "tensor")
    return jax.shard_map(
        per_device,
        mesh=mesh,
        in_specs=(both,) * 6 + (P("sample"), P("sample"), both),
        out_specs=(both, both),
        check_vma=False,
    )
```

```python
import functools

import jax
import jax.numpy as jnp
from jax import lax
from jax.experimental import pallas as pl
from jax.experimental.pallas import tpu as pltpu
from jax.sharding import PartitionSpec as P

HD = 128
HEADS = 8
ROWS = 128
SCALE = HD ** (-0.5) * 1.4426950408889634
ORDERS = (((4, 12, 16, 48), (12, 4, 48, 16)), ((16, 48, 4, 12), (48, 16, 12, 4)))
VMEM = pl.BlockSpec(memory_space=pltpu.VMEM)
SMEM = pl.BlockSpec(memory_space=pltpu.SMEM)


def slot_table(me):
    there = jnp.arange(16, dtype=jnp.int32)
    apart = there ^ (me >> 2)
    low_x, high_x = apart & 1, (apart >> 1) & 1
    low_y, high_y = (apart >> 2) & 1, (apart >> 3) & 1
    used = {4: low_x ^ high_x, 12: high_x, 16: low_y ^ high_y, 48: high_y}
    rows = []
    for rc in range(2):
        for piece in range(2):
            first, second = [
                sum(used[mask] << step for step, mask in enumerate(order))
                for order in ORDERS[piece]]
            rows.append(jnp.where((me & 1) == rc, first, second))
    return jnp.concatenate(rows)


def slot_of(info, rc, piece, there):
    return info[4 + (rc * 2 + piece) * 16 + there]


def take(halves, slot):
    low = slot & 7
    return jnp.where(slot > 7, halves[1][low], halves[0][low])


def swap(x, masks):
    masks = masks if isinstance(masks, tuple) else (masks, masks)
    return lax.ppermute(x, "sample", [(s, s ^ masks[s & 1]) for s in range(64)])


def swap_tensor(x, masks):
    pairs = [(s * 4 + t, s * 4 + (t ^ masks[s & 1])) for s in range(64) for t in range(4)]
    return lax.ppermute(x, ("sample", "tensor"), pairs)


def after(x, *others):
    return lax.optimization_barrier((x, *others))[0]


def step_masks(piece, step):
    return (ORDERS[piece][0][step], ORDERS[piece][1][step])


def gather_step(pieces, step):
    return [swap(piece, step_masks(i, step)) for i, piece in enumerate(pieces)]


def join(pieces, came):
    return [jnp.concatenate([a, b], axis=0) for a, b in zip(pieces, came)]


def score_head(q, h, keys):
    return lax.dot_general(
        q[:, h * HD:(h + 1) * HD], keys, (((1,), (1,)), ((), ())),
        preferred_element_type=jnp.float32)


def add_values(acc, h, exps, shrink, values):
    fresh = jnp.dot(exps, values, preferred_element_type=jnp.float32)
    if shrink is not None:
        fresh = acc[h] * jnp.concatenate([shrink, shrink], axis=1) + fresh
    acc[h] = fresh


def attend_kernel(is_prompt, first, count, info, q, own_k, own_v, *refs):
    blocks, (out, top, acc) = refs[:4], refs[4:]
    me = info[0]
    row = lax.broadcasted_iota(jnp.int32, (ROWS, ROWS), 0)
    ahead_by = row - lax.broadcasted_iota(jnp.int32, (ROWS, ROWS), 1)

    def absorb(pair, opening):
        begin = 8 * (me >> 5 if is_prompt else info[1]) + 2 * pair
        keys, values, floors = [], [], []
        for there in (begin, begin + 1):
            for rc in range(2):
                for rz in range(2):
                    both = blocks[rc * 2 + rz][slot_of(info, rc, rz, there)]
                    keys.append(both[:, :HD])
                    values.append(both[:, HD:])
                    later = there * 4 + ((me ^ (rz * 2 + rc)) & 3) - me
                    floors.append(later * ROWS if is_prompt and opening else None)
        if opening and not is_prompt:
            keys.append(own_k[...])
            values.append(own_v[...])
            floors.append(0)
        keys = jnp.concatenate(keys, axis=0)
        values = jnp.concatenate(values, axis=0)
        values = jnp.concatenate([values, jnp.ones(values.shape, jnp.bfloat16)], axis=1)
        ready = [score_head(q, first, keys), score_head(q, first + 1, keys)]
        behind = None
        for h in range(count):
            scores = ready.pop(0)
            if h + 2 < count:
                ready.append(score_head(q, first + h + 2, keys))
            parts = [scores[:, i * ROWS:(i + 1) * ROWS] for i in range(len(floors))]
            parts = [
                part if floor is None else jnp.where(ahead_by >= floor, part, -1e30)
                for floor, part in zip(floors, parts)]
            new = jnp.max(functools.reduce(jnp.maximum, parts), axis=1, keepdims=True)
            if opening:
                new = jnp.broadcast_to(new, (ROWS, HD))
                shrink = None
            else:
                old = top[h]
                new = jnp.maximum(old, new)
                shrink = jnp.exp2((old - new) * SCALE)
            top[h] = new
            exps = jnp.concatenate(
                [jnp.exp2((part - new) * SCALE).astype(jnp.bfloat16) for part in parts], axis=1)
            if behind is not None:
                add_values(acc, h - 1, *behind, values)
            behind = exps, shrink
        add_values(acc, count - 1, *behind, values)

    if is_prompt:
        last = (me & 31) >> 3
        absorb(last, True)
        lax.fori_loop(0, last, lambda i, c: (absorb(i, False), c)[1], 0)
    else:
        for i in range(4):
            absorb(i, i == 0)
    core, low_z = me & 1, (me >> 1) & 1
    for h in range(count):
        result = acc[h][:, :HD] / acc[h][:, HD:]
        if not is_prompt:
            result = jnp.where(row < info[2], result, 0.0)
        result = jnp.where(core == 0, result, pltpu.roll(result, HD // 2, 1))
        place = pl.multiple_of((h ^ low_z) * HD, HD)
        out[:, pl.ds(place, HD)] = result.astype(jnp.bfloat16)


def attend(is_prompt, first, count, info, q, own_k, own_v, blocks):
    return pl.pallas_call(
        functools.partial(attend_kernel, is_prompt, first, count),
        out_shape=jax.ShapeDtypeStruct((ROWS, count * HD), jnp.bfloat16),
        in_specs=[SMEM] + [VMEM] * (3 + len(blocks)),
        out_specs=VMEM,
        scratch_shapes=[
            pltpu.VMEM((count, ROWS, HD), jnp.float32),
            pltpu.VMEM((count, ROWS, 2 * HD), jnp.float32),
        ],
        compiler_params=pltpu.CompilerParams(vmem_limit_bytes=12 << 20),
        name="attend_%s_%d" % ("prompt" if is_prompt else "suffix", first),
    )(info, q, own_k, own_v, *blocks)


def project_kernel(info, a_p, a_s, near_s, mixed, far_p, *refs):
    weights, (out_p, out_s) = refs[:8], refs[8:]
    core, tensor = info[0] & 1, info[3]
    near = jnp.where(core == 0, 1, 3)
    pieces = [
        (quarter, jnp.concatenate(rows, axis=0)) for quarter, rows in (
            (tensor, (a_p[...], a_s[...])),
            (tensor ^ near, (far_p[0], near_s[...])),
            (tensor ^ near ^ 2, (mixed[2], mixed[0])),
            (tensor ^ 2, (far_p[1], mixed[1])))]
    for piece in range(2):
        lanes = slice(piece * 1024, (piece + 1) * 1024)
        sums = None
        for quarter, rows in pieces:
            held = []
            for x in range(4):
                there = quarter * 4 + x
                found = [
                    take(weights[rc * 4 + piece * 2:rc * 4 + piece * 2 + 2],
                         slot_of(info, rc, piece, there)) for rc in range(2)]
                for rz in range(2):
                    held += [found[0][rz], found[1][rz]]
            part = jnp.dot(
                rows, jnp.concatenate(held, axis=0), preferred_element_type=jnp.float32)
            sums = part if sums is None else sums + part
        out_p[:, lanes] = sums[:ROWS].astype(jnp.bfloat16)
        out_s[:, lanes] = sums[ROWS:].astype(jnp.bfloat16)


def project(info, heads, weights):
    args = [info, *heads, *weights]
    return pl.pallas_call(
        project_kernel,
        out_shape=[jax.ShapeDtypeStruct((ROWS, 2048), jnp.bfloat16)] * 2,
        in_specs=[SMEM] + [VMEM] * (len(args) - 1),
        out_specs=[VMEM] * 2,
        compiler_params=pltpu.CompilerParams(vmem_limit_bytes=24 << 20),
        name="project",
    )(*args)


def per_device(
    prompt_q, prompt_k, prompt_v, suffix_q, suffix_k, suffix_v, prompt_of, suffix_len, out_weight
):
    me = lax.axis_index("sample").astype(jnp.int32)
    info = jnp.concatenate([
        jnp.stack([me, prompt_of[0], suffix_len[0], lax.axis_index("tensor").astype(jnp.int32)]),
        slot_table(me)])

    other_k, other_v = swap(prompt_k, 2), swap(prompt_v, 2)
    own = lax.optimization_barrier(jnp.concatenate([prompt_k, prompt_v], axis=1))
    kv = [own[None], jnp.concatenate([other_k, other_v], axis=1)[None]]
    others = swap(after(out_weight, other_k), 2)
    kv = join(kv, gather_step(kv, 0))
    kv = join(kv, gather_step(kv, 1))
    others, info, out_weight, _ = lax.optimization_barrier((others, info, out_weight, kv[0]))
    w = [jnp.stack([part[:, lanes] for part in (out_weight, others)])[None]
         for lanes in (slice(0, 1024), slice(1024, 2048))]
    w_came = gather_step(w, 0)
    kv = join(kv, gather_step([after(a, *w) for a in kv], 2))
    w = join(w, w_came)
    w_came = gather_step(w, 1)
    came = gather_step(kv, 3)
    kv_mate = [swap(a, 1) for a in kv]
    came_mate = [swap(a, 1) for a in came]
    blocks = [*join(kv, came), *join(kv_mate, came_mate)]

    a_s = attend(False, 0, 4, info, suffix_q, suffix_k, suffix_v, blocks)
    a_s, suffix_q, prompt_q, *w_came = lax.optimization_barrier(
        (a_s, suffix_q, prompt_q, *w_came))
    more = attend(False, 4, 4, info, suffix_q, suffix_k, suffix_v, blocks)
    a_s = jnp.concatenate([a_s, more], axis=1)
    w = join(w, w_came)
    w_3 = gather_step(w, 2)
    near_s = swap_tensor(a_s, (1, 3))
    a_p = attend(True, 0, 8, info, after(prompt_q, *w), prompt_k, prompt_v, blocks)
    a_s, near_s, a_p = lax.optimization_barrier((a_s, near_s, a_p))
    mixed = swap_tensor(jnp.stack([a_s, near_s, a_p]), (3, 1))
    w = join(w, [after(a, a_p) for a in w_3])
    w_came = gather_step(w, 3)
    far_p = swap_tensor(jnp.stack([a_p, mixed[2]]), (1, 3))
    w_mate = [swap(a, 1) for a in w]
    w_came = [after(a, mixed) for a in w_came]
    w_came_mate = [swap(w_came[0], 1), swap(after(w_came[1], far_p), 1)]
    weights = [w[0], w_came[0], w[1], w_came[1],
               w_mate[0], w_came_mate[0], w_mate[1], w_came_mate[1]]
    return tuple(project(info, [a_p, a_s, near_s, mixed, far_p], weights))


def solution(mesh):
    both = P("sample", "tensor")
    return jax.shard_map(
        per_device,
        mesh=mesh,
        in_specs=(both,) * 6 + (P("sample"), P("sample"), both),
        out_specs=(both, both),
        check_vma=False,
    )
```
